32 devices in a mesh: dp: 4 (over z), tm: 2 (over core), rows: 4 (over y, x).
Axes of the slice: x: 2, y: 2, z: 4, core: 2. Of those that a mesh axis runs over, the one named last changes fastest.
Arguments:
- latent: bfloat16 [4, 4, 8, 176, 256], P('dp', 'tm', 'rows'), may hold values from -12 to 12, as said below
- gamma: float32 [256], replicated, may hold values from 0.1 to 1.9
- beta: float32 [256], replicated, may hold values from -3 to 3
- weight: bfloat16 [3, 3, 3, 256, 256], replicated, may hold values from -0.078125 to 0.078125
- bias: float32 [256], replicated, may hold values from -3 to 3
- cotangent: bfloat16 [4, 4, 8, 176, 256], P('dp', 'tm', 'rows'), may hold values from -0.039794922 to 0.039794922
Outputs:
- output: bfloat16 [4, 4, 8, 176, 256], P('dp', 'tm', 'rows')
- weight_grad: float32 [2304, 256], P(('tm', 'rows'))
The draws below stay inside these ranges and needn't reach their ends.
Inputs may be any that keep to these rules, and one draw needn't show every extreme that they name: `latent`: feature values, with each clip's group variance at least 0.5.
All inputs are finite; a program needn't handle non-finite values.
Results may differ from the reference program's by a relative error of at most 0.0029.
Values may be sent and summed in bfloat16 or wider, within the bound.
No kernel may reach another device: no remote copies, remote signals or barrier semaphores. Data moves between devices by JAX's collectives and lax.ppermute only.
A program may use at most 64 MiB of HBM per device.

```python
import jax
import jax.numpy as jnp
from jax import lax

CH = 256
GROUPS = 32
WID = 176
CLIPS = 4
FRAMES = 4
HEIGHT = 8


def draw_latent(key, part):
    key_base = jax.random.fold_in(key, 0)
    rowpos = jnp.arange(HEIGHT, dtype=jnp.float32) / max(HEIGHT - 1, 1)
    framepos = jnp.arange(FRAMES, dtype=jnp.float32) / max(FRAMES - 1, 1)
    shape = (CLIPS, FRAMES, HEIGHT, WID, CH)
    base = jnp.clip(jax.random.normal(key_base, shape, jnp.float32), -4.0, 4.0)
    growth = jnp.exp(jnp.log(3.0) * 0.5 * (rowpos[None, :] + framepos[:, None]))
    return (base * growth[None, :, :, None, None]).astype(jnp.bfloat16)


def level_of(stream_key, dims, cuts, smallest, largest):
    factor_of = 1.0
    for axis_at, parts in cuts:
        steps = jax.random.uniform(jax.random.fold_in(jax.random.fold_in(stream_key, 6), axis_at), (parts,), jnp.float32, smallest / len(cuts), largest / len(cuts))
        factor_of = factor_of * jnp.repeat(jnp.exp(steps), dims[axis_at] // parts).reshape((-1,) + (1,) * (len(dims) - 1 - axis_at))
    return factor_of


def noise(key, shape, width, reach, cuts=(), kind=jnp.bfloat16):
    loudness = level_of(key, shape, cuts, -0.22, 0.18) if cuts else 1.0
    entries = jax.random.normal(key, shape, jnp.float32) * width * loudness
    return jnp.minimum(jnp.maximum(entries, -reach), reach).astype(kind)


def setup_inputs(seed: int = 0) -> dict:
    seeds = jax.random.split(jax.random.key(seed), 7)
    return {
        "latent": draw_latent(jax.random.fold_in(seeds[6], 71), 0),
        "gamma": jnp.clip(1.0 + 0.18 * jax.random.normal(seeds[1], (CH,), jnp.float32), 0.1, 1.9),
        "beta": noise(seeds[2], (CH,), 0.5, 3.0, (), jnp.float32),
        "weight": noise(seeds[3], (3, 3, 3, CH, CH), (27 * CH) ** -0.5, 0.078125),
        "bias": noise(seeds[4], (CH,), 0.5, 3.0, (), jnp.float32),
        "cotangent": noise(seeds[5], (CLIPS, FRAMES, HEIGHT, WID, CH), ((CLIPS * FRAMES * HEIGHT * WID) ** -0.5), 0.039794922, ((0, 4), (1, 2), (2, 4))),
    }


def reference(latent, gamma, beta, weight, bias, cotangent):
    latent_f = latent.astype(jnp.float32)
    nclip, nframe, nheight, nwidth, nchan = latent_f.shape
    grouped = latent_f.reshape(nclip, nframe * nheight * nwidth, GROUPS, nchan // GROUPS)
    mean = lax.optimization_barrier(jnp.mean(grouped, axis=(1, 3), keepdims=True))
    centered = grouped - mean
    var = lax.optimization_barrier(jnp.mean(centered * centered, axis=(1, 3), keepdims=True))
    normed = (centered * lax.rsqrt(var + 1e-06)).reshape(latent_f.shape) * gamma + beta
    act = jax.nn.silu(normed).astype(jnp.bfloat16)
    padded = jnp.concatenate([act[:, :1], act[:, :1], act], axis=1)
    padded = jnp.pad(padded, ((0, 0), (0, 0), (1, 1), (1, 1), (0, 0)))
    padded_f = padded.astype(jnp.float32)
    kernel_f = weight.astype(jnp.float32)
    grads_f = cotangent.astype(jnp.float32)

    def per_clip(pair):
        clip, grad = pair
        flat_grad = grad.reshape(-1, nchan)
        total = jnp.zeros((nframe * nheight * nwidth, nchan), jnp.float32)
        pieces = []
        for offset_t in range(3):
            for offset_h in range(3):
                for offset_w in range(3):
                    window = clip[offset_t:offset_t + nframe, offset_h:offset_h + nheight, offset_w:offset_w + nwidth].reshape(-1, nchan)
                    total = total + jnp.dot(window, kernel_f[offset_t, offset_h, offset_w], precision=lax.Precision.HIGHEST)
                    if offset_t == 0:
                        pieces.append(jnp.dot(window.T, flat_grad, precision=lax.Precision.HIGHEST))
        return (total.reshape(nframe, nheight, nwidth, nchan), jnp.stack(pieces))
    conv, grads = lax.map(per_clip, (padded_f, grads_f))
    output = (latent_f + bias + conv).astype(jnp.bfloat16)
    weight_grad = lax.optimization_barrier(jnp.sum(grads, axis=0)).reshape(9 * nchan, nchan)
    return (output, weight_grad)
```

```python
import functools

import jax
import jax.numpy as jnp
from jax import lax
from jax.experimental import pallas as pl
from jax.experimental.pallas import tpu as pltpu
from jax.sharding import PartitionSpec as P

GROUPS = 32
BF16 = jnp.bfloat16
F32 = jnp.float32
VMEM_LIMIT = 40 * 1024 * 1024


def call(kernel, outs, ins, scratch=(), flops=0, nbytes=0, trans=0, name=None):
    specs = [
        pl.BlockSpec(memory_space=pltpu.SMEM)
        if a.dtype == jnp.int32
        else pl.BlockSpec(memory_space=pltpu.VMEM)
        for a in ins
    ]
    return pl.pallas_call(
        kernel,
        out_shape=outs,
        in_specs=specs,
        out_specs=jax.tree.map(lambda _: pl.BlockSpec(memory_space=pltpu.VMEM), outs),
        scratch_shapes=list(scratch),
        compiler_params=pltpu.CompilerParams(vmem_limit_bytes=VMEM_LIMIT),
        cost_estimate=pl.CostEstimate(flops=flops, bytes_accessed=nbytes, transcendentals=trans),
        name=name,
    )(*ins)


def stats_kernel(own_ref, other_ref, out_ref):
    rows, chans = own_ref.shape
    step = 88
    total = jnp.zeros((8, chans), F32)
    squares = jnp.zeros((8, chans), F32)
    for ref in (own_ref, other_ref):
        for at in range(0, rows, step):
            x = ref[at : at + step, :].astype(F32).reshape(step // 8, 8, chans)
            total = total + jnp.sum(x, axis=0)
            squares = squares + jnp.sum(x * x, axis=0)
    out_ref[0:8, :] = total
    out_ref[8:16, :] = squares


def shift_rows(x, by):
    zero = jnp.zeros((1, x.shape[1]), x.dtype)
    if by == 1:
        return jnp.concatenate([x[1:], zero], axis=0)
    if by == -1:
        return jnp.concatenate([zero, x[:-1]], axis=0)
    return x


def cot_kernel(where_ref, own_ref, other_ref, out_ref):
    _, height, width, chans = own_ref.shape
    is_late = where_ref[0] == 1
    for h in range(height):
        a0 = own_ref[0, h].astype(F32)
        a1 = own_ref[1, h].astype(F32)
        b0 = other_ref[0, h].astype(F32)
        b1 = other_ref[1, h].astype(F32)
        first = a0 + b0 + jnp.where(is_late, b1, a1)
        last = jnp.where(is_late, a1, b1)
        high = first.astype(BF16).astype(F32)
        low = first - high
        for term, value in enumerate((high, low, last)):
            for kw in range(3):
                out_ref[kw, term, h] = shift_rows(value, 1 - kw).astype(BF16)


def group_sum(x, per_group):
    chans = x.shape[1]
    lane = lax.broadcasted_iota(jnp.int32, x.shape, 1)
    step = 1
    while step < per_group:
        up = pltpu.roll(x, step, 1)
        down = pltpu.roll(x, chans - step, 1)
        x = x + jnp.where((lane & step) != 0, up, down)
        step *= 2
    return x


def activate(x, scale, shift):
    v = x.astype(F32) * scale + shift
    return v * (0.5 + 0.5 * jnp.tanh(0.5 * v))


def grad_kernel(count, n_stats, n_pieces, rows_out, *refs):
    where_ref = refs[0]
    stats = refs[1 : 1 + n_stats]
    (gamma_ref, beta_ref, own_ref, other_ref, own_low, own_high, other_low, other_high, cots_ref) = refs[
        1 + n_stats : 10 + n_stats
    ]
    act_ref, norm_ref = refs[10 + n_stats : 12 + n_stats]
    pieces = refs[12 + n_stats : 12 + n_stats + n_pieces]
    wg_ref = refs[12 + n_stats + n_pieces]
    late = where_ref[0]
    is_late = late == 1
    frames, height, width, chans = own_ref.shape
    sums = stats[0][...]
    for ref in stats[1:]:
        sums = sums + ref[...]
    total = jnp.sum(sums[0:8], axis=0, keepdims=True)
    squares = jnp.sum(sums[8:16], axis=0, keepdims=True)
    both = group_sum(jnp.concatenate([total, squares] + [total] * 6, axis=0), chans // GROUPS) / count
    mean = both[0:1]
    var = both[1:2] - mean * mean
    scale = lax.rsqrt(var + 1e-06) * gamma_ref[...]
    shift = beta_ref[...] - mean * scale
    norm_ref[0:1, :] = scale
    norm_ref[1:2, :] = shift
    norm_ref[2:8, :] = jnp.zeros((6, chans), F32)
    keep_low = (where_ref[1] != 0).astype(F32)
    keep_high = (where_ref[2] != 0).astype(F32)
    for f in range(frames):
        low = jnp.where(is_late, other_low[f], own_low[f])
        act_ref[f, 0] = (activate(low, scale, shift) * keep_low).astype(BF16)
        for h in range(height):
            x = jnp.where(is_late, other_ref[f, h], own_ref[f, h])
            act_ref[f, h + 1] = activate(x, scale, shift).astype(BF16)
        high = jnp.where(is_late, other_high[f], own_high[f])
        act_ref[f, height + 1] = (activate(high, scale, shift) * keep_high).astype(BF16)

    contract = (((0,), (0,)), ((), ()))
    terms = 3 * height * width

    def stack(kh):
        a0 = act_ref[0, pl.ds(kh, height)].reshape(height * width, chans)
        a1 = act_ref[1, pl.ds(kh, height)].reshape(height * width, chans)
        return jnp.concatenate([a0, a0, a1], axis=0)

    def cots(kw):
        return cots_ref[kw].reshape(terms, chans)

    half = chans // 2
    outer = stack(2 * late)
    base = pl.multiple_of(late * (chans + half), half)
    for kw in range(3):
        wg_ref[pl.ds(base + kw * chans, chans), :] = lax.dot_general(
            outer, cots(kw), contract, preferred_element_type=F32
        )
    middle = stack(1)
    base = pl.multiple_of(3 * chans - late * (5 * half), half)
    wg_ref[pl.ds(base, chans), :] = lax.dot_general(middle, cots(2 * late), contract, preferred_element_type=F32)
    lanes = jnp.where(is_late, middle[:, half:], middle[:, :half])
    base = pl.multiple_of((1 - late) * (4 * chans), half)
    wg_ref[pl.ds(base, half), :] = lax.dot_general(lanes, cots(1), contract, preferred_element_type=F32)
    for k, ref in enumerate(pieces):
        start = pl.multiple_of(where_ref[3 + k], 16)
        ref[...] = wg_ref[pl.ds(start, rows_out), :].astype(ref.dtype)


def conv_kernel(
    where_ref, norm_ref, act_ref, own_ref, own_low, own_high, weight_ref, bias_ref, out_ref, planes, acc
):
    late = where_ref[0]
    frames, height, width, chans = own_ref.shape
    scale = norm_ref[0:1, :]
    shift = norm_ref[1:2, :]
    keep_low = (where_ref[1] != 0).astype(F32)
    keep_high = (where_ref[2] != 0).astype(F32)
    planes[0] = act_ref[0]
    planes[1] = act_ref[late]
    for f in range(frames):
        planes[frames + f, 0] = (activate(own_low[f], scale, shift) * keep_low).astype(BF16)
        for h in range(height):
            planes[frames + f, h + 1] = activate(own_ref[f, h], scale, shift).astype(BF16)
        planes[frames + f, height + 1] = (activate(own_high[f], scale, shift) * keep_high).astype(BF16)
    for f in range(frames):
        for kw in range(3):
            total = None
            for kt in range(3):
                for kh in range(3):
                    lhs = planes[f + kt, kh : kh + height].reshape(height * width, chans)
                    part = jnp.dot(lhs, weight_ref[kt, kh, kw], preferred_element_type=F32)
                    total = part if total is None else total + part
            acc[kw] = total.reshape(height, width, chans)
        for h in range(height):
            value = own_ref[f, h].astype(F32) + bias_ref[...]
            value = value + acc[1, h] + shift_rows(acc[0, h], -1) + shift_rows(acc[2, h], 1)
            out_ref[f, h] = value.astype(BF16)


def body(dp, rows, latent, gamma, beta, weight, bias, cotangent):
    nclip, frames, height, width, chans = latent.shape
    lat = latent[0]
    cot = cotangent[0]
    swap = [(0, 1), (1, 0)]
    clip = lax.axis_index("dp")
    late = lax.axis_index("tm")
    band = lax.axis_index("rows")
    count = frames * height * width * (chans // GROUPS) * 2 * rows
    size = frames * height * width * chans

    other = lax.ppermute(lat, "tm", swap)
    other_cot = lax.ppermute(cot, "tm", swap)
    own_low = lax.ppermute(lat[:, height - 1], "rows", [(i, i + 1) for i in range(rows - 1)])
    own_high = lax.ppermute(lat[:, 0], "rows", [(i + 1, i) for i in range(rows - 1)])
    other_low = lax.ppermute(own_low, "tm", [(0, 1)])
    other_high = lax.ppermute(own_high, "tm", [(0, 1)])

    sums = call(
        stats_kernel,
        jax.ShapeDtypeStruct((16, chans), F32),
        (lat.reshape(-1, chans), other.reshape(-1, chans)),
        flops=6 * size,
        nbytes=4 * size,
        name="stats",
    )
    small = rows == 4 and dp == 4
    if small:
        stats = [sums] + [lax.ppermute(sums, "rows", [(i, i ^ k) for i in range(4)]) for k in (1, 2, 3)]
    else:
        stats = [lax.psum(sums, "rows")]

    half = 9 * chans // 2
    if small:
        piece = half // 8
        order = [(dz, dr) for dz in (0, 1) for dr in range(4)]
        starts = [(band ^ dr) * (2 * piece) + ((clip ^ dz) & 1) * piece for dz, dr in order]
        kinds = [F32] + [BF16] * 7
    else:
        piece = half
        starts = [jnp.int32(0)]
        kinds = [F32]
    where = jnp.stack([late, (band != 0).astype(jnp.int32), (band != rows - 1).astype(jnp.int32)] + starts).astype(
        jnp.int32
    )
    cots = call(
        cot_kernel,
        jax.ShapeDtypeStruct((3, 3, height, width, chans), BF16),
        (where, cot, other_cot),
        flops=10 * size,
        nbytes=14 * size,
        name="cots",
    )
    act, norm, *parts = call(
        functools.partial(grad_kernel, count, len(stats), len(kinds), piece),
        [
            jax.ShapeDtypeStruct((frames, height + 2, width, chans), BF16),
            jax.ShapeDtypeStruct((8, chans), F32),
        ]
        + [jax.ShapeDtypeStruct((piece, chans), k) for k in kinds],
        (where, *stats, gamma.reshape(1, -1), beta.reshape(1, -1), lat, other, own_low, own_high, other_low, other_high, cots),
        scratch=[pltpu.VMEM((half, chans), F32)],
        flops=2 * half * 3 * height * width * chans,
        nbytes=20 * size,
        trans=2 * size,
        name="grad",
    )
    output = call(
        conv_kernel,
        jax.ShapeDtypeStruct((frames, height, width, chans), BF16),
        (where, norm, act, lat, own_low, own_high, weight, bias.reshape(1, -1)),
        scratch=[
            pltpu.VMEM((4, height + 2, width, chans), BF16),
            pltpu.VMEM((3, height, width, chans), F32),
        ],
        flops=2 * 27 * size * chans,
        nbytes=4 * size + 2 * weight.size,
        trans=2 * size,
        name="conv",
    )
    if small:
        got = [
            lax.ppermute(
                p,
                ("dp", "rows"),
                [(z * 4 + r, (z ^ dz) * 4 + (r ^ dr)) for z in range(4) for r in range(4)],
            )
            for p, (dz, dr) in zip(parts[1:], order[1:])
        ]
        total = parts[0]
        for g in got:
            total = total + g.astype(F32)
        total = total.astype(BF16)
        by = [total] + [lax.ppermute(total, "dp", [(z, z ^ k) for z in range(4)]) for k in (1, 2, 3)]
        by = [b.astype(F32) for b in by]
        mine = by[0] + by[2]
        theirs = by[1] + by[3]
        even = clip % 2 == 0
        grad = jnp.concatenate([jnp.where(even, mine, theirs), jnp.where(even, theirs, mine)], axis=0)
    else:
        grad = lax.psum(lax.psum_scatter(parts[0], "rows", scatter_dimension=0, tiled=True), "dp")
    return output[None], grad


def solution(mesh):
    placed = (
        P("dp", "tm", "rows", None, None),
        P(),
        P(),
        P(),
        P(),
        P("dp", "tm", "rows", None, None),
    )
    return jax.shard_map(
        functools.partial(body, mesh.shape["dp"], mesh.shape["rows"]),
        mesh=mesh,
        in_specs=placed,
        out_specs=(P("dp", "tm", "rows", None, None), P(("tm", "rows"), None)),
        check_vma=False,
    )
```

```python
import functools

import jax
import jax.numpy as jnp
from jax import lax
from jax.experimental import pallas as pl
from jax.experimental.pallas import tpu as pltpu
from jax.sharding import PartitionSpec as P

GROUPS = 32
BF16 = jnp.bfloat16
F32 = jnp.float32
VMEM_LIMIT = 24 * 1024 * 1024


def call(kernel, outs, ins, scratch=(), flops=0, nbytes=0, trans=0, name=None, outside=(), limit=VMEM_LIMIT):
    specs = [
        pl.BlockSpec(memory_space=pltpu.HBM if k in outside else pltpu.SMEM if a.dtype == jnp.int32 else pltpu.VMEM)
        for k, a in enumerate(ins)
    ]
    return pl.pallas_call(
        kernel,
        out_shape=outs,
        in_specs=specs,
        out_specs=jax.tree.map(lambda _: pl.BlockSpec(memory_space=pltpu.VMEM), outs),
        scratch_shapes=list(scratch),
        compiler_params=pltpu.CompilerParams(vmem_limit_bytes=limit),
        cost_estimate=pl.CostEstimate(flops=flops, bytes_accessed=nbytes, transcendentals=trans),
        name=name,
    )(*ins)


def channel_sums(ref):
    frames, height, width, chans = ref.shape
    total = jnp.zeros((8, chans), F32)
    squares = jnp.zeros((8, chans), F32)
    for f in range(frames):
        for h in range(height):
            x = ref[f, h].astype(F32).reshape(width // 8, 8, chans)
            total = total + jnp.sum(x, axis=0)
            squares = squares + jnp.sum(x * x, axis=0)
    return jnp.concatenate([total, squares], axis=0)


def own_kernel(own_ref, copy_ref, sums_ref):
    copy_ref[...] = own_ref[...]
    sums_ref[...] = channel_sums(own_ref)


def prep_kernel(where_ref, own_sums_ref, own_ref, other_ref, sums_ref, early_ref, late_ref):
    frames, height, width, chans = own_ref.shape
    is_late = where_ref[0] == 1
    row = where_ref[3]
    sums = own_sums_ref[...] + channel_sums(other_ref)
    sums_ref[...] = sums
    for f in range(frames):
        mine = own_ref[f, row]
        other = other_ref[f, row]
        early_ref[f * width : (f + 1) * width, :] = jnp.where(is_late, other, mine)
        late_ref[f * width : (f + 1) * width, :] = jnp.where(is_late, mine, other)
    for k in range(3):
        term = sums.astype(BF16)
        early_ref[frames * width + 16 * k : frames * width + 16 * (k + 1), :] = term
        sums = sums - term.astype(F32)


def shift_rows(x, by):
    zero = jnp.zeros((1, x.shape[1]), x.dtype)
    if by == 1:
        return jnp.concatenate([x[1:], zero], axis=0)
    if by == -1:
        return jnp.concatenate([zero, x[:-1]], axis=0)
    return x


def cot_kernel(where_ref, own_ref, other_ref, out_ref):
    _, height, width, chans = own_ref.shape
    is_late = where_ref[0] == 1
    for h in range(height):
        a0 = own_ref[0, h].astype(F32)
        a1 = own_ref[1, h].astype(F32)
        b0 = other_ref[0, h].astype(F32)
        b1 = other_ref[1, h].astype(F32)
        first = a0 + b0 + jnp.where(is_late, b1, a1)
        last = jnp.where(is_late, a1, b1)
        high = first.astype(BF16).astype(F32)
        low = first - high
        for term, value in enumerate((high, low, last)):
            for kw in range(3):
                out_ref[kw, term, h] = shift_rows(value, 1 - kw).astype(BF16)


def group_sum(x, per_group):
    chans = x.shape[1]
    lane = lax.broadcasted_iota(jnp.int32, x.shape, 1)
    step = 1
    while step < per_group:
        up = pltpu.roll(x, step, 1)
        down = pltpu.roll(x, chans - step, 1)
        x = x + jnp.where((lane & step) != 0, up, down)
        step *= 2
    return x


def activate(x, scale, shift):
    v = x.astype(F32) * scale + shift
    return v * (0.5 + 0.5 * jnp.tanh(0.5 * v))


def grad_kernel(count, decode, n_stats, n_pieces, rows_out, *refs):
    where_ref = refs[0]
    stats = refs[1 : 1 + n_stats]
    params_ref, own_ref, other_ref, near_ref, far_ref, cots_ref = refs[1 + n_stats : 7 + n_stats]
    act_ref, norm_ref = refs[7 + n_stats : 9 + n_stats]
    pieces = refs[9 + n_stats : 9 + n_stats + n_pieces]
    wg_ref = refs[9 + n_stats + n_pieces]
    late = where_ref[0]
    is_late = late == 1
    low_is_near = where_ref[4] == 1
    frames, height, width, chans = own_ref.shape
    sums = stats[0][...]
    for ref in stats[1:]:
        sums = sums + ref[...]
    if decode:
        for ref in (near_ref, far_ref):
            base = frames * width
            terms = [ref[base + 16 * k : base + 16 * (k + 1), :].astype(F32) for k in range(3)]
            sums = sums + (terms[0] + (terms[1] + terms[2]))
    total = jnp.sum(sums[0:8], axis=0, keepdims=True)
    squares = jnp.sum(sums[8:16], axis=0, keepdims=True)
    both = group_sum(jnp.concatenate([total, squares] + [total] * 6, axis=0), chans // GROUPS) / count
    mean = both[0:1]
    var = both[1:2] - mean * mean
    scale = lax.rsqrt(var + 1e-06) * params_ref[0:1, :]
    shift = params_ref[1:2, :] - mean * scale
    norm_ref[0:1, :] = scale
    norm_ref[1:2, :] = shift
    norm_ref[2:8, :] = jnp.zeros((6, chans), F32)
    keep_low = (where_ref[1] != 0).astype(F32)
    keep_high = (where_ref[2] != 0).astype(F32)
    for f in range(frames):
        near = near_ref[f * width : (f + 1) * width, :]
        far = far_ref[f * width : (f + 1) * width, :]
        low = jnp.where(low_is_near, near, far)
        act_ref[f, 0] = (activate(low, scale, shift) * keep_low).astype(BF16)
        for h in range(height):
            x = jnp.where(is_late, other_ref[f, h], own_ref[f, h])
            act_ref[f, h + 1] = activate(x, scale, shift).astype(BF16)
        high = jnp.where(low_is_near, far, near)
        act_ref[f, height + 1] = (activate(high, scale, shift) * keep_high).astype(BF16)

    contract = (((0,), (0,)), ((), ()))
    terms = 3 * height * width

    def stack(kh):
        a0 = act_ref[0, pl.ds(kh, height)].reshape(height * width, chans)
        a1 = act_ref[1, pl.ds(kh, height)].reshape(height * width, chans)
        return jnp.concatenate([a0, a0, a1], axis=0)

    def cots(kw):
        return cots_ref[kw].reshape(terms, chans)

    half = chans // 2
    outer = stack(2 * late)
    base = pl.multiple_of(late * (chans + half), half)
    for kw in range(3):
        wg_ref[pl.ds(base + kw * chans, chans), :] = lax.dot_general(
            outer, cots(kw), contract, preferred_element_type=F32
        )
    middle = stack(1)
    base = pl.multiple_of(3 * chans - late * (5 * half), half)
    wg_ref[pl.ds(base, chans), :] = lax.dot_general(middle, cots(2 * late), contract, preferred_element_type=F32)
    lanes = jnp.where(is_late, middle[:, half:], middle[:, :half])
    base = pl.multiple_of((1 - late) * (4 * chans), half)
    wg_ref[pl.ds(base, half), :] = lax.dot_general(lanes, cots(1), contract, preferred_element_type=F32)
    for k, ref in enumerate(pieces):
        start = pl.multiple_of(where_ref[5 + k], 16)
        ref[...] = wg_ref[pl.ds(start, rows_out), :].astype(ref.dtype)


def conv_kernel(where_ref, norm_ref, act_ref, own_ref, near_ref, far_ref, weight_hbm, params_ref, out_ref, planes, acc, weight_ref, sems):
    copies = [pltpu.make_async_copy(weight_hbm.at[:, :, kw], weight_ref.at[:, :, kw], sems.at[kw]) for kw in range(3)]
    for c in copies:
        c.start()
    late = where_ref[0]
    low_is_near = where_ref[4] == 1
    frames, height, width, chans = own_ref.shape
    planes[0] = act_ref[0]
    planes[1] = act_ref[late]

    @pl.when(late == 0)
    def _():
        planes[2] = act_ref[0]
        planes[3] = act_ref[1]

    @pl.when(late == 1)
    def _():
        scale = norm_ref[0:1, :]
        shift = norm_ref[1:2, :]
        keep_low = (where_ref[1] != 0).astype(F32)
        keep_high = (where_ref[2] != 0).astype(F32)
        for f in range(frames):
            near = near_ref[f * width : (f + 1) * width, :]
            far = far_ref[f * width : (f + 1) * width, :]
            low = jnp.where(low_is_near, near, far)
            high = jnp.where(low_is_near, far, near)
            planes[frames + f, 0] = (activate(low, scale, shift) * keep_low).astype(BF16)
            for h in range(height):
                planes[frames + f, h + 1] = activate(own_ref[f, h], scale, shift).astype(BF16)
            planes[frames + f, height + 1] = (activate(high, scale, shift) * keep_high).astype(BF16)

    for kw in range(3):
        copies[kw].wait()
        for f in range(frames):
            total = None
            for kt in range(3):
                for kh in range(3):
                    lhs = planes[f + kt, kh : kh + height].reshape(height * width, chans)
                    part = jnp.dot(lhs, weight_ref[kt, kh, kw], preferred_element_type=F32)
                    total = part if total is None else total + part
            total = total.reshape(height, width, chans)
            for h in range(height):
                if kw == 0:
                    acc[f, h] = shift_rows(total[h], -1)
                elif kw == 1:
                    acc[f, h] = acc[f, h] + total[h]
                else:
                    value = own_ref[f, h].astype(F32) + params_ref[2:3, :] + acc[f, h] + shift_rows(total[h], 1)
                    out_ref[f, h] = value.astype(BF16)


def body(dp, rows, latent, gamma, beta, weight, bias, cotangent):
    nclip, frames, height, width, chans = latent.shape
    lat = latent[0]
    cot = cotangent[0]
    swap = [(0, 1), (1, 0)]
    clip = lax.axis_index("dp")
    late = lax.axis_index("tm")
    band = lax.axis_index("rows")
    count = frames * height * width * (chans // GROUPS) * 2 * rows
    size = frames * height * width * chans
    small = rows == 4 and dp == 4

    odd = band % 2
    beyond = [(r - 1) % rows if r % 2 == 0 else (r + 1) % rows for r in range(rows)]
    joint = [(r, r ^ 1) for r in range(rows)] + [(rows + r, rows + beyond[r]) for r in range(rows)]
    low_is_near = (odd ^ late) if rows > 1 else late
    edge_row = jnp.where(low_is_near == 1, 0, height - 1)
    head = [late, (band != 0), (band != rows - 1), edge_row, low_is_near]

    other = lax.ppermute(lat, "tm", swap)
    other_cot = lax.ppermute(cot, "tm", swap)
    lat, own_sums = call(
        own_kernel,
        [jax.ShapeDtypeStruct(lat.shape, lat.dtype), jax.ShapeDtypeStruct((16, chans), F32)],
        (lat,),
        flops=3 * size,
        nbytes=4 * size,
        name="own",
    )
    half = 9 * chans // 2
    if small:
        piece = half // 8
        order = [(0, 0), (0, 2), (1, 3), (1, 2), (1, 0), (1, 1), (0, 3), (0, 1)]
        starts = [(band ^ dr) * (2 * piece) + ((clip ^ dz) & 1) * piece for dz, dr in order]
        kinds = [F32] + [BF16] * 7
    else:
        piece = half
        starts = [jnp.int32(0)]
        kinds = [F32]
    where = jnp.stack([jnp.asarray(v).astype(jnp.int32) for v in head + starts])
    sums, early_rims, late_rims = call(
        prep_kernel,
        [
            jax.ShapeDtypeStruct((16, chans), F32),
            jax.ShapeDtypeStruct((frames * width + 48, chans), BF16),
            jax.ShapeDtypeStruct((frames * width, chans), BF16),
        ],
        (where, own_sums, lat, other),
        flops=3 * size,
        nbytes=6 * size,
        name="prep",
    )
    near = lax.ppermute(early_rims, ("tm", "rows"), joint)
    if small:
        stats = [sums, lax.ppermute(sums, "rows", [(r, r ^ 2) for r in range(rows)])]
    else:
        stats = [lax.psum(sums, "rows")]
    params = jnp.stack([gamma, beta, bias] + [jnp.zeros_like(bias)] * 5)
    cots = call(
        cot_kernel,
        jax.ShapeDtypeStruct((3, 3, height, width, chans), BF16),
        (where, cot, other_cot),
        flops=10 * size,
        nbytes=14 * size,
        name="cots",
    )
    near_late = lax.ppermute(late_rims, ("tm", "rows"), joint)
    near, cots, params, stats[-1] = lax.optimization_barrier((near, cots, params, stats[-1]))
    far = lax.ppermute(near, "tm", swap)
    far_late = lax.ppermute(near_late, "tm", swap)
    act, norm, *parts = call(
        functools.partial(grad_kernel, count, small, len(stats), len(kinds), piece),
        [
            jax.ShapeDtypeStruct((frames, height + 2, width, chans), BF16),
            jax.ShapeDtypeStruct((8, chans), F32),
        ]
        + [jax.ShapeDtypeStruct((piece, chans), k) for k in kinds],
        (where, *stats, params, lat, other, near, far, cots),
        scratch=[pltpu.VMEM((half, chans), F32)],
        flops=2 * half * 3 * height * width * chans,
        nbytes=20 * size,
        trans=2 * size,
        name="grad",
    )
    def convolve():
        return call(
            conv_kernel,
            jax.ShapeDtypeStruct((frames, height, width, chans), BF16),
            (where, norm, act, lat, near_late, far_late, weight, params),
            scratch=[
                pltpu.VMEM((4, height + 2, width, chans), BF16),
                pltpu.VMEM((frames, height, width, chans), F32),
                pltpu.VMEM(weight.shape, weight.dtype),
                pltpu.SemaphoreType.DMA((3,)),
            ],
            flops=2 * 27 * size * chans,
            nbytes=4 * size + 2 * weight.size,
            trans=2 * size,
            name="conv",
            outside=(6,),
            limit=51 * 1024 * 1024,
        )

    if small:
        got = [
            lax.ppermute(
                p,
                ("dp", "rows"),
                [(z * 4 + r, (z ^ dz) * 4 + (r ^ dr)) for z in range(4) for r in range(4)],
            )
            for p, (dz, dr) in zip(parts[1:], order[1:])
        ]
        total = parts[0]
        for g in got:
            total = total + g.astype(F32)
        total, far_late = lax.optimization_barrier((total.astype(BF16), far_late))
        by = [total] + [lax.ppermute(total, "dp", [(z, z ^ k) for z in range(4)]) for k in (1, 2, 3)]
        output = convolve()
        *by, output = lax.optimization_barrier((*by, output))
        by = [b.astype(F32) for b in by]
        mine = by[0] + by[2]
        theirs = by[1] + by[3]
        even = clip % 2 == 0
        grad = jnp.concatenate([jnp.where(even, mine, theirs), jnp.where(even, theirs, mine)], axis=0)
    else:
        output = convolve()
        grad = lax.psum(lax.psum_scatter(parts[0], "rows", scatter_dimension=0, tiled=True), "dp")
    return output[None], grad


def solution(mesh):
    placed = (
        P("dp", "tm", "rows", None, None),
        P(),
        P(),
        P(),
        P(),
        P("dp", "tm", "rows", None, None),
    )
    return jax.shard_map(
        functools.partial(body, mesh.shape["dp"], mesh.shape["rows"]),
        mesh=mesh,
        in_specs=placed,
        out_specs=(P("dp", "tm", "rows", None, None), P(("tm", "rows"), None)),
        check_vma=False,
    )
```

```python
import functools

import jax
import jax.numpy as jnp
from jax import lax
from jax.experimental import pallas as pl
from jax.experimental.pallas import tpu as pltpu
from jax.sharding import PartitionSpec as P

GROUPS = 32
BF16 = jnp.bfloat16
F32 = jnp.float32
VMEM_LIMIT = 24 * 1024 * 1024


def call(kernel, outs, ins, scratch=(), flops=0, nbytes=0, trans=0, name=None, outside=(), limit=VMEM_LIMIT):
    specs = [
        pl.BlockSpec(memory_space=pltpu.HBM if k in outside else pltpu.SMEM if a.dtype == jnp.int32 else pltpu.VMEM)
        for k, a in enumerate(ins)
    ]
    return pl.pallas_call(
        kernel,
        out_shape=outs,
        in_specs=specs,
        out_specs=jax.tree.map(lambda _: pl.BlockSpec(memory_space=pltpu.VMEM), outs),
        scratch_shapes=list(scratch),
        compiler_params=pltpu.CompilerParams(vmem_limit_bytes=limit),
        cost_estimate=pl.CostEstimate(flops=flops, bytes_accessed=nbytes, transcendentals=trans),
        name=name,
    )(*ins)


def channel_sums(ref):
    frames, height, width, chans = ref.shape
    total = jnp.zeros((8, chans), F32)
    squares = jnp.zeros((8, chans), F32)
    for f in range(frames):
        for h in range(height):
            x = ref[f, h].astype(F32).reshape(width // 8, 8, chans)
            total = total + jnp.sum(x, axis=0)
            squares = squares + jnp.sum(x * x, axis=0)
    return jnp.concatenate([total, squares], axis=0)


def own_kernel(own_ref, copy_ref, sums_ref):
    copy_ref[...] = own_ref[...]
    sums_ref[...] = channel_sums(own_ref)


def prep_kernel(where_ref, own_sums_ref, own_ref, other_ref, sums_ref, early_ref, late_ref):
    frames, height, width, chans = own_ref.shape
    is_late = where_ref[0] == 1
    row = where_ref[3]
    sums = own_sums_ref[...] + channel_sums(other_ref)
    sums_ref[...] = sums
    for f in range(frames):
        mine = own_ref[f, row]
        other = other_ref[f, row]
        early_ref[f * width : (f + 1) * width, :] = jnp.where(is_late, other, mine)
        late_ref[f * width : (f + 1) * width, :] = jnp.where(is_late, mine, other)
    for k in range(3):
        term = sums.astype(BF16)
        early_ref[frames * width + 16 * k : frames * width + 16 * (k + 1), :] = term
        sums = sums - term.astype(F32)


def shift_rows(x, by):
    zero = jnp.zeros((1, x.shape[1]), x.dtype)
    if by == 1:
        return jnp.concatenate([x[1:], zero], axis=0)
    if by == -1:
        return jnp.concatenate([zero, x[:-1]], axis=0)
    return x


def cot_kernel(where_ref, own_ref, other_ref, out_ref):
    _, height, width, chans = own_ref.shape
    is_late = where_ref[0] == 1
    for h in range(height):
        a0 = own_ref[0, h].astype(F32)
        a1 = own_ref[1, h].astype(F32)
        b0 = other_ref[0, h].astype(F32)
        b1 = other_ref[1, h].astype(F32)
        first = a0 + b0 + jnp.where(is_late, b1, a1)
        last = jnp.where(is_late, a1, b1)
        high = first.astype(BF16).astype(F32)
        low = first - high
        for term, value in enumerate((high, low, last)):
            for kw in range(3):
                out_ref[kw, term, h] = shift_rows(value, 1 - kw).astype(BF16)


def group_sum(x, per_group):
    chans = x.shape[1]
    lane = lax.broadcasted_iota(jnp.int32, x.shape, 1)
    step = 1
    while step < per_group:
        up = pltpu.roll(x, step, 1)
        down = pltpu.roll(x, chans - step, 1)
        x = x + jnp.where((lane & step) != 0, up, down)
        step *= 2
    return x


def activate(x, scale, shift):
    v = x.astype(F32) * scale + shift
    return v * (0.5 + 0.5 * jnp.tanh(0.5 * v))


def grad_kernel(count, decode, n_stats, n_pieces, rows_out, *refs):
    where_ref = refs[0]
    stats = refs[1 : 1 + n_stats]
    params_ref, own_ref, other_ref, near_ref, far_sums_ref, cots_ref = refs[1 + n_stats : 7 + n_stats]
    act_ref, norm_ref = refs[7 + n_stats : 9 + n_stats]
    pieces = refs[9 + n_stats : 9 + n_stats + n_pieces]
    wg_ref = refs[9 + n_stats + n_pieces]
    late = where_ref[0]
    is_late = late == 1
    frames, height, width, chans = own_ref.shape
    sums = stats[0][...]
    for ref in stats[1:]:
        sums = sums + ref[...]
    if decode:
        for ref, base in ((near_ref, frames * width), (far_sums_ref, 0)):
            terms = [ref[base + 16 * k : base + 16 * (k + 1), :].astype(F32) for k in range(3)]
            sums = sums + (terms[0] + (terms[1] + terms[2]))
    total = jnp.sum(sums[0:8], axis=0, keepdims=True)
    squares = jnp.sum(sums[8:16], axis=0, keepdims=True)
    both = group_sum(jnp.concatenate([total, squares] + [total] * 6, axis=0), chans // GROUPS) / count
    mean = both[0:1]
    var = both[1:2] - mean * mean
    scale = lax.rsqrt(var + 1e-06) * params_ref[0:1, :]
    shift = params_ref[1:2, :] - mean * scale
    norm_ref[0:1, :] = scale
    norm_ref[1:2, :] = shift
    norm_ref[2:8, :] = jnp.zeros((6, chans), F32)
    keep = (where_ref[1] != 0).astype(F32)
    for f in range(frames):
        near = near_ref[f * width : (f + 1) * width, :]
        act_ref[f, late * (height + 1)] = (activate(near, scale, shift) * keep).astype(BF16)
        act_ref[f, (1 - late) * (height + 1)] = jnp.zeros((width, chans), BF16)
        for h in range(height):
            x = jnp.where(is_late, other_ref[f, h], own_ref[f, h])
            act_ref[f, h + 1] = activate(x, scale, shift).astype(BF16)

    contract = (((0,), (0,)), ((), ()))
    terms = 3 * height * width

    def stack(kh):
        a0 = act_ref[0, pl.ds(kh, height)].reshape(height * width, chans)
        a1 = act_ref[1, pl.ds(kh, height)].reshape(height * width, chans)
        return jnp.concatenate([a0, a0, a1], axis=0)

    def cots(kw):
        return cots_ref[kw].reshape(terms, chans)

    half = chans // 2
    outer = stack(2 * late)
    base = pl.multiple_of(late * (chans + half), half)
    for kw in range(3):
        wg_ref[pl.ds(base + kw * chans, chans), :] = lax.dot_general(
            outer, cots(kw), contract, preferred_element_type=F32
        )
    middle = stack(1)
    base = pl.multiple_of(3 * chans - late * (5 * half), half)
    wg_ref[pl.ds(base, chans), :] = lax.dot_general(middle, cots(2 * late), contract, preferred_element_type=F32)
    lanes = jnp.where(is_late, middle[:, half:], middle[:, :half])
    base = pl.multiple_of((1 - late) * (4 * chans), half)
    wg_ref[pl.ds(base, half), :] = lax.dot_general(lanes, cots(1), contract, preferred_element_type=F32)
    for k, ref in enumerate(pieces):
        start = pl.multiple_of(where_ref[4 + k], 16)
        ref[...] = wg_ref[pl.ds(start, rows_out), :].astype(ref.dtype)


def conv_kernel(
    where_ref, norm_ref, act_ref, own_ref, far_ref, near_late, far_late, weight_hbm, params_ref, out_ref, planes, acc, weight_ref, sems
):
    taps = [(kt, kh) for kt in range(3) for kh in range(3)]
    copies = [
        pltpu.make_async_copy(weight_hbm.at[kt, kh], weight_ref.at[kt, kh], sems.at[k]) for k, (kt, kh) in enumerate(taps)
    ]
    for c in copies:
        c.start()
    late = where_ref[0]
    frames, height, width, chans = own_ref.shape
    scale = norm_ref[0:1, :]
    shift = norm_ref[1:2, :]
    keep_near = (where_ref[1] != 0).astype(F32)
    keep_far = (where_ref[2] != 0).astype(F32)

    def rim(ref, f, keep):
        return (activate(ref[f * width : (f + 1) * width, :], scale, shift) * keep).astype(BF16)

    @pl.when(late == 0)
    def _():
        for f in range(frames):
            planes[2 + f] = act_ref[f]
            planes[2 + f, height + 1] = rim(far_ref, f, keep_far)
        for k in range(2):
            planes[k] = planes[2]

    @pl.when(late == 1)
    def _():
        for f in range(frames):
            planes[f] = act_ref[f]
            planes[f, 0] = rim(far_ref, f, keep_far)
            planes[2 + f, 0] = rim(far_late, f, keep_far)
            for h in range(height):
                planes[2 + f, h + 1] = activate(own_ref[f, h], scale, shift).astype(BF16)
            planes[2 + f, height + 1] = rim(near_late, f, keep_near)

    for kt in range(3):
        for c in copies[3 * kt : 3 * kt + 3]:
            c.wait()
        for f in range(frames):
            for kw in range(3):
                total = None
                for kh in range(3):
                    lhs = planes[f + kt, kh : kh + height].reshape(height * width, chans)
                    part = jnp.dot(lhs, weight_ref[kt, kh, kw], preferred_element_type=F32)
                    total = part if total is None else total + part
                total = total.reshape(height, width, chans)
                acc[f, kw] = total if kt == 0 else acc[f, kw] + total
    for f in range(frames):
        for h in range(height):
            value = own_ref[f, h].astype(F32) + params_ref[2:3, :]
            value = value + acc[f, 1, h] + shift_rows(acc[f, 0, h], -1) + shift_rows(acc[f, 2, h], 1)
            out_ref[f, h] = value.astype(BF16)


def body(dp, rows, latent, gamma, beta, weight, bias, cotangent):
    nclip, frames, height, width, chans = latent.shape
    lat = latent[0]
    cot = cotangent[0]
    swap = [(0, 1), (1, 0)]
    clip = lax.axis_index("dp")
    late = lax.axis_index("tm")
    band = lax.axis_index("rows")
    count = frames * height * width * (chans // GROUPS) * 2 * rows
    size = frames * height * width * chans
    small = rows == 4 and dp == 4

    joint = [(r, (r + 1) % rows) for r in range(rows)] + [(rows + r, rows + (r - 1) % rows) for r in range(rows)]
    keep_low, keep_high = (band != 0), (band != rows - 1)
    head = [
        late,
        jnp.where(late == 0, keep_low, keep_high),
        jnp.where(late == 0, keep_high, keep_low),
        jnp.where(late == 0, height - 1, 0),
    ]

    other = lax.ppermute(lat, "tm", swap)
    other_cot = lax.ppermute(cot, "tm", swap)
    lat, own_sums = call(
        own_kernel,
        [jax.ShapeDtypeStruct(lat.shape, lat.dtype), jax.ShapeDtypeStruct((16, chans), F32)],
        (lat,),
        flops=3 * size,
        nbytes=4 * size,
        name="own",
    )
    half = 9 * chans // 2
    if small:
        piece = half // 8
        order = [(0, 0), (0, 2), (1, 3), (1, 2), (1, 0), (1, 1), (0, 3), (0, 1)]
        starts = [(band ^ dr) * (2 * piece) + ((clip ^ dz) & 1) * piece for dz, dr in order]
        kinds = [F32] + [BF16] * 7
    else:
        piece = half
        starts = [jnp.int32(0)]
        kinds = [F32]
    where = jnp.stack([jnp.asarray(v).astype(jnp.int32) for v in head + starts])
    sums, early_rims, late_rims = call(
        prep_kernel,
        [
            jax.ShapeDtypeStruct((16, chans), F32),
            jax.ShapeDtypeStruct((frames * width + 48, chans), BF16),
            jax.ShapeDtypeStruct((frames * width, chans), BF16),
        ],
        (where, own_sums, lat, other),
        flops=3 * size,
        nbytes=6 * size,
        name="prep",
    )
    near = lax.ppermute(early_rims, ("tm", "rows"), joint)
    if small:
        stats = [
            sums,
            lax.ppermute(sums, "rows", [(r, (r + 2) % rows) for r in range(rows)]),
        ]
    else:
        stats = [lax.psum(sums, "rows")]
    params = jnp.stack([gamma, beta, bias] + [jnp.zeros_like(bias)] * 5)
    cots = call(
        cot_kernel,
        jax.ShapeDtypeStruct((3, 3, height, width, chans), BF16),
        (where, cot, other_cot),
        flops=10 * size,
        nbytes=14 * size,
        name="cots",
    )
    cots, params, late_rims, stats[-1] = lax.optimization_barrier((cots, params, late_rims, stats[-1]))
    near_late = lax.ppermute(late_rims, ("tm", "rows"), joint)
    near, stats[-1], cots = lax.optimization_barrier((near, stats[-1], cots))
    far_sums = lax.ppermute(near[frames * width :], "tm", swap)
    act, norm, *parts = call(
        functools.partial(grad_kernel, count, small, len(stats), len(kinds), piece),
        [
            jax.ShapeDtypeStruct((frames, height + 2, width, chans), BF16),
            jax.ShapeDtypeStruct((8, chans), F32),
        ]
        + [jax.ShapeDtypeStruct((piece, chans), k) for k in kinds],
        (where, *stats, params, lat, other, near, far_sums, cots),
        scratch=[pltpu.VMEM((half, chans), F32)],
        flops=2 * half * 3 * height * width * chans,
        nbytes=20 * size,
        trans=2 * size,
        name="grad",
    )
    def convolve(far, near_late, far_late):
        return call(
            conv_kernel,
            jax.ShapeDtypeStruct((frames, height, width, chans), BF16),
            (where, norm, act, lat, far, near_late, far_late, weight, params),
            scratch=[
                pltpu.VMEM((4, height + 2, width, chans), BF16),
                pltpu.VMEM((frames, 3, height, width, chans), F32),
                pltpu.VMEM(weight.shape, weight.dtype),
                pltpu.SemaphoreType.DMA((9,)),
            ],
            flops=2 * 27 * size * chans,
            nbytes=4 * size + 2 * weight.size,
            trans=2 * size,
            name="conv",
            outside=(7,),
            limit=51 * 1024 * 1024,
        )

    if small:
        got = [
            lax.ppermute(
                p,
                ("dp", "rows"),
                [(z * 4 + r, (z ^ dz) * 4 + (r ^ dr)) for z in range(4) for r in range(4)],
            )
            for p, (dz, dr) in zip(parts[1:], order[1:])
        ]
        near, near_late, total = lax.optimization_barrier((near, near_late, parts[0]))
        far = lax.ppermute(near, "tm", swap)
        far_late = lax.ppermute(near_late, "tm", swap)
        for g in got:
            total = total + g.astype(F32)
        total, far, far_late = lax.optimization_barrier((total.astype(BF16), far, far_late))
        by = [total] + [lax.ppermute(total, "dp", [(z, z ^ k) for z in range(4)]) for k in (1, 2, 3)]
        output = convolve(far, near_late, far_late)
        *by, output = lax.optimization_barrier((*by, output))
        by = [b.astype(F32) for b in by]
        mine = by[0] + by[2]
        theirs = by[1] + by[3]
        even = clip % 2 == 0
        grad = jnp.concatenate([jnp.where(even, mine, theirs), jnp.where(even, theirs, mine)], axis=0)
    else:
        far = lax.ppermute(near, "tm", swap)
        output = convolve(far, near_late, lax.ppermute(near_late, "tm", swap))
        grad = lax.psum(lax.psum_scatter(parts[0], "rows", scatter_dimension=0, tiled=True), "dp")
    return output[None], grad


def solution(mesh):
    placed = (
        P("dp", "tm", "rows", None, None),
        P(),
        P(),
        P(),
        P(),
        P("dp", "tm", "rows", None, None),
    )
    return jax.shard_map(
        functools.partial(body, mesh.shape["dp"], mesh.shape["rows"]),
        mesh=mesh,
        in_specs=placed,
        out_specs=(P("dp", "tm", "rows", None, None), P(("tm", "rows"), None)),
        check_vma=False,
    )
```

```python
import functools

import jax
import jax.numpy as jnp
from jax import lax
from jax.experimental import pallas as pl
from jax.experimental.pallas import tpu as pltpu
from jax.sharding import PartitionSpec as P

GROUPS = 32
BF16 = jnp.bfloat16
F32 = jnp.float32
VMEM_LIMIT = 24 * 1024 * 1024


def call(kernel, outs, ins, scratch=(), flops=0, nbytes=0, trans=0, name=None, outside=(), limit=VMEM_LIMIT):
    specs = [
        pl.BlockSpec(memory_space=pltpu.HBM if k in outside else pltpu.SMEM if a.dtype == jnp.int32 else pltpu.VMEM)
        for k, a in enumerate(ins)
    ]
    return pl.pallas_call(
        kernel,
        out_shape=outs,
        in_specs=specs,
        out_specs=jax.tree.map(lambda _: pl.BlockSpec(memory_space=pltpu.VMEM), outs),
        scratch_shapes=list(scratch),
        compiler_params=pltpu.CompilerParams(vmem_limit_bytes=limit),
        cost_estimate=pl.CostEstimate(flops=flops, bytes_accessed=nbytes, transcendentals=trans),
        name=name,
    )(*ins)


def channel_sums(ref):
    frames, height, width, chans = ref.shape
    total = jnp.zeros((8, chans), F32)
    squares = jnp.zeros((8, chans), F32)
    for f in range(frames):
        for h in range(height):
            x = ref[f, h].astype(F32).reshape(width // 8, 8, chans)
            total = total + jnp.sum(x, axis=0)
            squares = squares + jnp.sum(x * x, axis=0)
    return jnp.concatenate([total, squares], axis=0)


def own_kernel(own_ref, copy_ref, sums_ref):
    copy_ref[...] = own_ref[...]
    sums_ref[...] = channel_sums(own_ref)


def prep_kernel(where_ref, own_sums_ref, own_ref, other_ref, sums_ref, early_ref, late_ref):
    frames, height, width, chans = own_ref.shape
    is_late = where_ref[0] == 1
    row = where_ref[3]
    sums = own_sums_ref[...] + channel_sums(other_ref)
    sums_ref[...] = sums
    for f in range(frames):
        mine = own_ref[f, row]
        other = other_ref[f, row]
        early_ref[f * width : (f + 1) * width, :] = jnp.where(is_late, other, mine)
        late_ref[f * width : (f + 1) * width, :] = jnp.where(is_late, mine, other)
    for k in range(3):
        term = sums.astype(BF16)
        early_ref[frames * width + 16 * k : frames * width + 16 * (k + 1), :] = term
        sums = sums - term.astype(F32)


def shift_rows(x, by):
    zero = jnp.zeros((1, x.shape[1]), x.dtype)
    if by == 1:
        return jnp.concatenate([x[1:], zero], axis=0)
    if by == -1:
        return jnp.concatenate([zero, x[:-1]], axis=0)
    return x


def cot_kernel(where_ref, own_ref, other_ref, out_ref):
    _, height, width, chans = own_ref.shape
    is_late = where_ref[0] == 1
    for h in range(height):
        a0 = own_ref[0, h].astype(F32)
        a1 = own_ref[1, h].astype(F32)
        b0 = other_ref[0, h].astype(F32)
        b1 = other_ref[1, h].astype(F32)
        first = a0 + b0 + jnp.where(is_late, b1, a1)
        last = jnp.where(is_late, a1, b1)
        high = first.astype(BF16).astype(F32)
        low = first - high
        for term, value in enumerate((high, low, last)):
            for kw in range(3):
                out_ref[kw, term, h] = shift_rows(value, 1 - kw).astype(BF16)


def group_sum(x, per_group):
    chans = x.shape[1]
    lane = lax.broadcasted_iota(jnp.int32, x.shape, 1)
    step = 1
    while step < per_group:
        up = pltpu.roll(x, step, 1)
        down = pltpu.roll(x, chans - step, 1)
        x = x + jnp.where((lane & step) != 0, up, down)
        step *= 2
    return x


def activate(x, scale, shift):
    v = x.astype(F32) * scale + shift
    return v * (0.5 + 0.5 * jnp.tanh(0.5 * v))


def grad_kernel(count, decode, n_stats, n_pieces, rows_out, *refs):
    where_ref = refs[0]
    stats = refs[1 : 1 + n_stats]
    params_ref, own_ref, other_ref, near_ref, far_sums_ref, cots_ref = refs[1 + n_stats : 7 + n_stats]
    act_ref, norm_ref = refs[7 + n_stats : 9 + n_stats]
    pieces = refs[9 + n_stats : 9 + n_stats + n_pieces]
    wg_ref = refs[9 + n_stats + n_pieces]
    late = where_ref[0]
    is_late = late == 1
    frames, height, width, chans = own_ref.shape
    sums = stats[0][...]
    for ref in stats[1:]:
        sums = sums + ref[...]
    if decode:
        for ref, base in ((near_ref, frames * width), (far_sums_ref, 0)):
            terms = [ref[base + 16 * k : base + 16 * (k + 1), :].astype(F32) for k in range(3)]
            sums = sums + (terms[0] + (terms[1] + terms[2]))
    total = jnp.sum(sums[0:8], axis=0, keepdims=True)
    squares = jnp.sum(sums[8:16], axis=0, keepdims=True)
    both = group_sum(jnp.concatenate([total, squares] + [total] * 6, axis=0), chans // GROUPS) / count
    mean = both[0:1]
    var = both[1:2] - mean * mean
    scale = lax.rsqrt(var + 1e-06) * params_ref[0:1, :]
    shift = params_ref[1:2, :] - mean * scale
    norm_ref[0:1, :] = scale
    norm_ref[1:2, :] = shift
    norm_ref[2:8, :] = jnp.zeros((6, chans), F32)
    keep = (where_ref[1] != 0).astype(F32)
    for f in range(frames):
        near = near_ref[f * width : (f + 1) * width, :]
        act_ref[f, late * (height + 1)] = (activate(near, scale, shift) * keep).astype(BF16)
        act_ref[f, (1 - late) * (height + 1)] = jnp.zeros((width, chans), BF16)
        for h in range(height):
            x = jnp.where(is_late, other_ref[f, h], own_ref[f, h])
            act_ref[f, h + 1] = activate(x, scale, shift).astype(BF16)

    contract = (((0,), (0,)), ((), ()))
    terms = 3 * height * width

    def stack(kh):
        a0 = act_ref[0, pl.ds(kh, height)].reshape(height * width, chans)
        a1 = act_ref[1, pl.ds(kh, height)].reshape(height * width, chans)
        return jnp.concatenate([a0, a0, a1], axis=0)

    def cots(kw):
        return cots_ref[kw].reshape(terms, chans)

    half = chans // 2
    outer = stack(2 * late)
    base = pl.multiple_of(late * (chans + half), half)
    for kw in range(3):
        wg_ref[pl.ds(base + kw * chans, chans), :] = lax.dot_general(
            outer, cots(kw), contract, preferred_element_type=F32
        )
    middle = stack(1)
    base = pl.multiple_of(3 * chans - late * (5 * half), half)
    wg_ref[pl.ds(base, chans), :] = lax.dot_general(middle, cots(2 * late), contract, preferred_element_type=F32)
    lanes = jnp.where(is_late, middle[:, half:], middle[:, :half])
    base = pl.multiple_of((1 - late) * (4 * chans), half)
    wg_ref[pl.ds(base, half), :] = lax.dot_general(lanes, cots(1), contract, preferred_element_type=F32)
    for k, ref in enumerate(pieces):
        start = pl.multiple_of(where_ref[4 + k], 16)
        ref[...] = wg_ref[pl.ds(start, rows_out), :].astype(ref.dtype)


def conv_kernel(
    where_ref, norm_ref, act_ref, own_ref, far_ref, near_late, far_late, weight_hbm, params_ref, first_ref, out_ref, planes, acc, weight_ref, sems
):
    taps = [(0, 2)] + [(kt, kh) for kt in (1, 2) for kh in range(3)]
    copies = [
        pltpu.make_async_copy(weight_hbm.at[kt, kh], weight_ref.at[k], sems.at[k]) for k, (kt, kh) in enumerate(taps)
    ]
    for c in copies:
        c.start()
    late = where_ref[0]
    frames, height, width, chans = own_ref.shape
    scale = norm_ref[0:1, :]
    shift = norm_ref[1:2, :]
    keep_near = (where_ref[1] != 0).astype(F32)
    keep_far = (where_ref[2] != 0).astype(F32)

    def rim(ref, f, keep):
        return (activate(ref[f * width : (f + 1) * width, :], scale, shift) * keep).astype(BF16)

    @pl.when(late == 0)
    def _():
        for f in range(frames):
            planes[2 + f] = act_ref[f]
            planes[2 + f, height + 1] = rim(far_ref, f, keep_far)
        for k in range(2):
            planes[k] = planes[2]

    @pl.when(late == 1)
    def _():
        for f in range(frames):
            planes[f] = act_ref[f]
            planes[f, 0] = rim(far_ref, f, keep_far)
            planes[2 + f, 0] = rim(far_late, f, keep_far)
            for h in range(height):
                planes[2 + f, h + 1] = activate(own_ref[f, h], scale, shift).astype(BF16)
            planes[2 + f, height + 1] = rim(near_late, f, keep_near)

    early = first_ref.shape[1]
    for kt, offsets in ((0, range(early)), (0, range(early, 3)), (1, range(3)), (2, range(3))):
        first = kt == 0 and offsets[0] == 0
        if not first:
            for kh in offsets:
                copies[3 * kt + kh - early].wait()
        for f in range(frames):
            for kw in range(3):
                total = None
                for kh in offsets:
                    lhs = planes[f + kt, kh : kh + height].reshape(height * width, chans)
                    taps_ref = first_ref.at[0, kh] if first else weight_ref.at[3 * kt + kh - early]
                    part = jnp.dot(lhs, taps_ref[kw], preferred_element_type=F32)
                    total = part if total is None else total + part
                total = total.reshape(height, width, chans)
                acc[f, kw] = total if first else acc[f, kw] + total
    for f in range(frames):
        for h in range(height):
            value = own_ref[f, h].astype(F32) + params_ref[2:3, :]
            value = value + acc[f, 1, h] + shift_rows(acc[f, 0, h], -1) + shift_rows(acc[f, 2, h], 1)
            out_ref[f, h] = value.astype(BF16)


def body(dp, rows, latent, gamma, beta, weight, bias, cotangent):
    nclip, frames, height, width, chans = latent.shape
    lat = latent[0]
    cot = cotangent[0]
    swap = [(0, 1), (1, 0)]
    clip = lax.axis_index("dp")
    late = lax.axis_index("tm")
    band = lax.axis_index("rows")
    count = frames * height * width * (chans // GROUPS) * 2 * rows
    size = frames * height * width * chans
    small = rows == 4 and dp == 4

    joint = [(r, (r + 1) % rows) for r in range(rows)] + [(rows + r, rows + (r - 1) % rows) for r in range(rows)]
    keep_low, keep_high = (band != 0), (band != rows - 1)
    head = [
        late,
        jnp.where(late == 0, keep_low, keep_high),
        jnp.where(late == 0, keep_high, keep_low),
        jnp.where(late == 0, height - 1, 0),
    ]

    other = lax.ppermute(lat, "tm", swap)
    other_cot = lax.ppermute(cot, "tm", swap)
    lat, own_sums = call(
        own_kernel,
        [jax.ShapeDtypeStruct(lat.shape, lat.dtype), jax.ShapeDtypeStruct((16, chans), F32)],
        (lat,),
        flops=3 * size,
        nbytes=4 * size,
        name="own",
    )
    half = 9 * chans // 2
    if small:
        piece = half // 8
        order = [(0, 0), (0, 2), (1, 3), (1, 2), (1, 0), (1, 1), (0, 3), (0, 1)]
        starts = [(band ^ dr) * (2 * piece) + ((clip ^ dz) & 1) * piece for dz, dr in order]
        kinds = [F32] + [BF16] * 7
    else:
        piece = half
        starts = [jnp.int32(0)]
        kinds = [F32]
    where = jnp.stack([jnp.asarray(v).astype(jnp.int32) for v in head + starts])
    sums, early_rims, late_rims = call(
        prep_kernel,
        [
            jax.ShapeDtypeStruct((16, chans), F32),
            jax.ShapeDtypeStruct((frames * width + 48, chans), BF16),
            jax.ShapeDtypeStruct((frames * width, chans), BF16),
        ],
        (where, own_sums, lat, other),
        flops=3 * size,
        nbytes=6 * size,
        name="prep",
    )
    near = lax.ppermute(early_rims, ("tm", "rows"), joint)
    if small:
        stats = [
            sums,
            lax.ppermute(sums, "rows", [(r, (r + 2) % rows) for r in range(rows)]),
        ]
    else:
        stats = [lax.psum(sums, "rows")]
    params = jnp.stack([gamma, beta, bias] + [jnp.zeros_like(bias)] * 5)
    cots = call(
        cot_kernel,
        jax.ShapeDtypeStruct((3, 3, height, width, chans), BF16),
        (where, cot, other_cot),
        flops=10 * size,
        nbytes=14 * size,
        name="cots",
    )
    cots, params, late_rims, stats[-1] = lax.optimization_barrier((cots, params, late_rims, stats[-1]))
    near_late = lax.ppermute(late_rims, ("tm", "rows"), joint)
    near, stats[-1], cots = lax.optimization_barrier((near, stats[-1], cots))
    far_sums = lax.ppermute(near[frames * width :], "tm", swap)
    act, norm, *parts = call(
        functools.partial(grad_kernel, count, small, len(stats), len(kinds), piece),
        [
            jax.ShapeDtypeStruct((frames, height + 2, width, chans), BF16),
            jax.ShapeDtypeStruct((8, chans), F32),
        ]
        + [jax.ShapeDtypeStruct((piece, chans), k) for k in kinds],
        (where, *stats, params, lat, other, near, far_sums, cots),
        scratch=[pltpu.VMEM((half, chans), F32)],
        flops=2 * half * 3 * height * width * chans,
        nbytes=20 * size,
        trans=2 * size,
        name="grad",
    )
    def convolve(far, near_late, far_late, first):
        return call(
            conv_kernel,
            jax.ShapeDtypeStruct((frames, height, width, chans), BF16),
            (where, norm, act, lat, far, near_late, far_late, weight, params, first),
            scratch=[
                pltpu.VMEM((4, height + 2, width, chans), BF16),
                pltpu.VMEM((frames, 3, height, width, chans), F32),
                pltpu.VMEM((7,) + weight.shape[2:], weight.dtype),
                pltpu.SemaphoreType.DMA((7,)),
            ],
            flops=2 * 27 * size * chans,
            nbytes=4 * size + 2 * weight.size,
            trans=2 * size,
            name="conv",
            outside=(7,),
            limit=50 * 1024 * 1024,
        )

    if small:
        got = [
            lax.ppermute(
                p,
                ("dp", "rows"),
                [(z * 4 + r, (z ^ dz) * 4 + (r ^ dr)) for z in range(4) for r in range(4)],
            )
            for p, (dz, dr) in zip(parts[1:], order[1:])
        ]
        near, near_late, total = lax.optimization_barrier((near, near_late, parts[0]))
        far = lax.ppermute(near, "tm", swap)
        far_late = lax.ppermute(near_late, "tm", swap)
        for g in got:
            total = total + g.astype(F32)
        total = total.astype(BF16)
        later, far, far_late, first = lax.optimization_barrier((total, far, far_late, weight[:1, :2]))
        by = [total] + [
            lax.ppermute(t, "dp", [(z, z ^ k) for z in range(4)]) for k, t in ((1, later), (2, total), (3, total))
        ]
        output = convolve(far, near_late, far_late, first)
        *by, output = lax.optimization_barrier((*by, output))
        by = [b.astype(F32) for b in by]
        mine = by[0] + by[2]
        theirs = by[1] + by[3]
        even = clip % 2 == 0
        grad = jnp.concatenate([jnp.where(even, mine, theirs), jnp.where(even, theirs, mine)], axis=0)
    else:
        far = lax.ppermute(near, "tm", swap)
        output = convolve(far, near_late, lax.ppermute(near_late, "tm", swap), weight[:1, :2])
        grad = lax.psum(lax.psum_scatter(parts[0], "rows", scatter_dimension=0, tiled=True), "dp")
    return output[None], grad


def solution(mesh):
    placed = (
        P("dp", "tm", "rows", None, None),
        P(),
        P(),
        P(),
        P(),
        P("dp", "tm", "rows", None, None),
    )
    return jax.shard_map(
        functools.partial(body, mesh.shape["dp"], mesh.shape["rows"]),
        mesh=mesh,
        in_specs=placed,
        out_specs=(P("dp", "tm", "rows", None, None), P(("tm", "rows"), None)),
        check_vma=False,
    )
```

```python
import functools

import jax
import jax.numpy as jnp
from jax import lax
from jax.experimental import pallas as pl
from jax.experimental.pallas import tpu as pltpu
from jax.sharding import PartitionSpec as P

GROUPS = 32
BF16 = jnp.bfloat16
F32 = jnp.float32
VMEM_LIMIT = 24 * 1024 * 1024


def call(kernel, outs, ins, scratch=(), flops=0, nbytes=0, trans=0, name=None, outside=(), limit=VMEM_LIMIT):
    specs = [
        pl.BlockSpec(memory_space=pltpu.HBM if k in outside else pltpu.SMEM if a.dtype == jnp.int32 else pltpu.VMEM)
        for k, a in enumerate(ins)
    ]
    return pl.pallas_call(
        kernel,
        out_shape=outs,
        in_specs=specs,
        out_specs=jax.tree.map(lambda _: pl.BlockSpec(memory_space=pltpu.VMEM), outs),
        scratch_shapes=list(scratch),
        compiler_params=pltpu.CompilerParams(vmem_limit_bytes=limit),
        cost_estimate=pl.CostEstimate(flops=flops, bytes_accessed=nbytes, transcendentals=trans),
        name=name,
    )(*ins)


def channel_sums(ref):
    frames, height, width, chans = ref.shape
    total = jnp.zeros((8, chans), F32)
    squares = jnp.zeros((8, chans), F32)
    for f in range(frames):
        for h in range(height):
            x = ref[f, h].astype(F32).reshape(width // 8, 8, chans)
            total = total + jnp.sum(x, axis=0)
            squares = squares + jnp.sum(x * x, axis=0)
    return jnp.concatenate([total, squares], axis=0)


def own_kernel(own_ref, copy_ref, sums_ref):
    copy_ref[...] = own_ref[...]
    sums_ref[...] = channel_sums(own_ref)


def prep_kernel(where_ref, own_sums_ref, own_ref, other_ref, sums_ref, early_ref, late_ref):
    frames, height, width, chans = own_ref.shape
    is_late = where_ref[0] == 1
    row = where_ref[3]
    sums = own_sums_ref[...] + channel_sums(other_ref)
    sums_ref[...] = sums
    for f in range(frames):
        mine = own_ref[f, row]
        other = other_ref[f, row]
        early_ref[f * width : (f + 1) * width, :] = jnp.where(is_late, other, mine)
        late_ref[f * width : (f + 1) * width, :] = jnp.where(is_late, mine, other)
    for k in range(3):
        term = sums.astype(BF16)
        early_ref[frames * width + 16 * k : frames * width + 16 * (k + 1), :] = term
        sums = sums - term.astype(F32)


def shift_rows(x, by):
    zero = jnp.zeros((1, x.shape[1]), x.dtype)
    if by == 1:
        return jnp.concatenate([x[1:], zero], axis=0)
    if by == -1:
        return jnp.concatenate([zero, x[:-1]], axis=0)
    return x


def cot_kernel(where_ref, own_ref, other_ref, out_ref):
    _, height, width, chans = own_ref.shape
    is_late = where_ref[0] == 1
    for h in range(height):
        a0 = own_ref[0, h].astype(F32)
        a1 = own_ref[1, h].astype(F32)
        b0 = other_ref[0, h].astype(F32)
        b1 = other_ref[1, h].astype(F32)
        first = a0 + b0 + jnp.where(is_late, b1, a1)
        last = jnp.where(is_late, a1, b1)
        high = first.astype(BF16).astype(F32)
        low = first - high
        for term, value in enumerate((high, low, last)):
            for kw in range(3):
                out_ref[kw, term, h] = shift_rows(value, 1 - kw).astype(BF16)


def group_sum(x, per_group):
    chans = x.shape[1]
    lane = lax.broadcasted_iota(jnp.int32, x.shape, 1)
    step = 1
    while step < per_group:
        up = pltpu.roll(x, step, 1)
        down = pltpu.roll(x, chans - step, 1)
        x = x + jnp.where((lane & step) != 0, up, down)
        step *= 2
    return x


def activate(x, scale, shift):
    v = x.astype(F32) * scale + shift
    return v * (0.5 + 0.5 * jnp.tanh(0.5 * v))


def grad_kernel(count, decode, n_stats, n_pieces, rows_out, *refs):
    where_ref = refs[0]
    stats = refs[1 : 1 + n_stats]
    params_ref, own_ref, other_ref, near_ref, far_sums_ref, cots_ref = refs[1 + n_stats : 7 + n_stats]
    act_ref, norm_ref = refs[7 + n_stats : 9 + n_stats]
    pieces = refs[9 + n_stats : 9 + n_stats + n_pieces]
    wg_ref = refs[9 + n_stats + n_pieces]
    late = where_ref[0]
    is_late = late == 1
    frames, height, width, chans = own_ref.shape
    sums = stats[0][...]
    for ref in stats[1:]:
        sums = sums + ref[...]
    if decode:
        for ref, base in ((near_ref, frames * width), (far_sums_ref, 0)):
            terms = [ref[base + 16 * k : base + 16 * (k + 1), :].astype(F32) for k in range(3)]
            sums = sums + (terms[0] + (terms[1] + terms[2]))
    total = jnp.sum(sums[0:8], axis=0, keepdims=True)
    squares = jnp.sum(sums[8:16], axis=0, keepdims=True)
    both = group_sum(jnp.concatenate([total, squares] + [total] * 6, axis=0), chans // GROUPS) / count
    mean = both[0:1]
    var = both[1:2] - mean * mean
    scale = lax.rsqrt(var + 1e-06) * params_ref[0:1, :]
    shift = params_ref[1:2, :] - mean * scale
    norm_ref[0:1, :] = scale
    norm_ref[1:2, :] = shift
    norm_ref[2:8, :] = jnp.zeros((6, chans), F32)
    keep = (where_ref[1] != 0).astype(F32)
    for f in range(frames):
        near = near_ref[f * width : (f + 1) * width, :]
        act_ref[f, late * (height + 1)] = (activate(near, scale, shift) * keep).astype(BF16)
        act_ref[f, (1 - late) * (height + 1)] = jnp.zeros((width, chans), BF16)
        for h in range(height):
            x = jnp.where(is_late, other_ref[f, h], own_ref[f, h])
            act_ref[f, h + 1] = activate(x, scale, shift).astype(BF16)

    contract = (((0,), (0,)), ((), ()))
    terms = 3 * height * width

    def stack(kh):
        a0 = act_ref[0, pl.ds(kh, height)].reshape(height * width, chans)
        a1 = act_ref[1, pl.ds(kh, height)].reshape(height * width, chans)
        return jnp.concatenate([a0, a0, a1], axis=0)

    def cots(kw):
        return cots_ref[kw].reshape(terms, chans)

    half = chans // 2
    outer = stack(2 * late)
    base = pl.multiple_of(late * (chans + half), half)
    for kw in range(3):
        wg_ref[pl.ds(base + kw * chans, chans), :] = lax.dot_general(
            outer, cots(kw), contract, preferred_element_type=F32
        )
    middle = stack(1)
    base = pl.multiple_of(3 * chans - late * (5 * half), half)
    wg_ref[pl.ds(base, chans), :] = lax.dot_general(middle, cots(2 * late), contract, preferred_element_type=F32)
    lanes = jnp.where(is_late, middle[:, half:], middle[:, :half])
    base = pl.multiple_of((1 - late) * (4 * chans), half)
    wg_ref[pl.ds(base, half), :] = lax.dot_general(lanes, cots(1), contract, preferred_element_type=F32)
    for k, ref in enumerate(pieces):
        start = pl.multiple_of(where_ref[4 + k], 16)
        ref[...] = wg_ref[pl.ds(start, rows_out), :].astype(ref.dtype)


def conv_kernel(
    where_ref, norm_ref, act_ref, own_ref, far_ref, near_late, far_late, weight_hbm, params_ref, first_ref, out_ref, planes, acc, weight_ref, sems
):
    taps = [(0, 2)] + [(kt, kh) for kt in (1, 2) for kh in range(3)]
    copies = [
        pltpu.make_async_copy(weight_hbm.at[kt, kh], weight_ref.at[k], sems.at[k]) for k, (kt, kh) in enumerate(taps)
    ]
    for c in copies:
        c.start()
    late = where_ref[0]
    frames, height, width, chans = own_ref.shape
    scale = norm_ref[0:1, :]
    shift = norm_ref[1:2, :]
    keep_near = (where_ref[1] != 0).astype(F32)
    keep_far = (where_ref[2] != 0).astype(F32)

    def rim(ref, f, keep):
        return (activate(ref[f * width : (f + 1) * width, :], scale, shift) * keep).astype(BF16)

    @pl.when(late == 0)
    def _():
        for f in range(frames):
            planes[2 + f] = act_ref[f]
            planes[2 + f, height + 1] = rim(far_ref, f, keep_far)
        for k in range(2):
            planes[k] = planes[2]

    @pl.when(late == 1)
    def _():
        for f in range(frames):
            planes[f] = act_ref[f]
            planes[f, 0] = rim(far_ref, f, keep_far)
            planes[2 + f, 0] = rim(far_late, f, keep_far)
            for h in range(height):
                planes[2 + f, h + 1] = activate(own_ref[f, h], scale, shift).astype(BF16)
            planes[2 + f, height + 1] = rim(near_late, f, keep_near)

    early = first_ref.shape[1]
    for kt, offsets in ((0, range(early)), (0, range(early, 3)), (1, range(3)), (2, range(3))):
        first = kt == 0 and offsets[0] == 0
        if not first:
            for kh in offsets:
                copies[3 * kt + kh - early].wait()
        for f in range(frames):
            for kw in range(3):
                total = None
                for kh in offsets:
                    lhs = planes[f + kt, kh : kh + height].reshape(height * width, chans)
                    taps_ref = first_ref.at[0, kh] if first else weight_ref.at[3 * kt + kh - early]
                    part = jnp.dot(lhs, taps_ref[kw], preferred_element_type=F32)
                    total = part if total is None else total + part
                total = total.reshape(height, width, chans)
                acc[f, kw] = total if first else acc[f, kw] + total
    for f in range(frames):
        for h in range(height):
            value = own_ref[f, h].astype(F32) + params_ref[2:3, :]
            value = value + acc[f, 1, h] + shift_rows(acc[f, 0, h], -1) + shift_rows(acc[f, 2, h], 1)
            out_ref[f, h] = value.astype(BF16)


def body(dp, rows, latent, gamma, beta, weight, bias, cotangent):
    nclip, frames, height, width, chans = latent.shape
    lat = latent[0]
    cot = cotangent[0]
    swap = [(0, 1), (1, 0)]
    clip = lax.axis_index("dp")
    late = lax.axis_index("tm")
    band = lax.axis_index("rows")
    count = frames * height * width * (chans // GROUPS) * 2 * rows
    size = frames * height * width * chans
    small = rows == 4 and dp == 4

    joint = [(r, (r + 1) % rows) for r in range(rows)] + [(rows + r, rows + (r - 1) % rows) for r in range(rows)]
    keep_low, keep_high = (band != 0), (band != rows - 1)
    head = [
        late,
        jnp.where(late == 0, keep_low, keep_high),
        jnp.where(late == 0, keep_high, keep_low),
        jnp.where(late == 0, height - 1, 0),
    ]

    other = lax.ppermute(lat, "tm", swap)
    other_cot = lax.ppermute(cot, "tm", swap)
    lat, own_sums = call(
        own_kernel,
        [jax.ShapeDtypeStruct(lat.shape, lat.dtype), jax.ShapeDtypeStruct((16, chans), F32)],
        (lat,),
        flops=3 * size,
        nbytes=4 * size,
        name="own",
    )
    half = 9 * chans // 2
    if small:
        piece = half // 8
        order = [(0, 0), (1, 3), (1, 0), (0, 1), (0, 2), (1, 2), (1, 1), (0, 3)]
        starts = [(band ^ dr) * (2 * piece) + ((clip ^ dz) & 1) * piece for dz, dr in order]
        kinds = [F32] + [BF16] * 7
    else:
        piece = half
        starts = [jnp.int32(0)]
        kinds = [F32]
    where = jnp.stack([jnp.asarray(v).astype(jnp.int32) for v in head + starts])
    sums, early_rims, late_rims = call(
        prep_kernel,
        [
            jax.ShapeDtypeStruct((16, chans), F32),
            jax.ShapeDtypeStruct((frames * width + 48, chans), BF16),
            jax.ShapeDtypeStruct((frames * width, chans), BF16),
        ],
        (where, own_sums, lat, other),
        flops=3 * size,
        nbytes=6 * size,
        name="prep",
    )
    near = lax.ppermute(early_rims, ("tm", "rows"), joint)
    if small:
        stats = [
            sums,
            lax.ppermute(sums, "rows", [(r, (r + 2) % rows) for r in range(rows)]),
        ]
    else:
        stats = [lax.psum(sums, "rows")]
    params = jnp.stack([gamma, beta, bias] + [jnp.zeros_like(bias)] * 5)
    cots = call(
        cot_kernel,
        jax.ShapeDtypeStruct((3, 3, height, width, chans), BF16),
        (where, cot, other_cot),
        flops=10 * size,
        nbytes=14 * size,
        name="cots",
    )
    cots, params, late_rims, stats[-1] = lax.optimization_barrier((cots, params, late_rims, stats[-1]))
    near_late = lax.ppermute(late_rims, ("tm", "rows"), joint)
    near, stats[-1], cots = lax.optimization_barrier((near, stats[-1], cots))
    far_sums = lax.ppermute(near[frames * width :], "tm", swap)
    act, norm, *parts = call(
        functools.partial(grad_kernel, count, small, len(stats), len(kinds), piece),
        [
            jax.ShapeDtypeStruct((frames, height + 2, width, chans), BF16),
            jax.ShapeDtypeStruct((8, chans), F32),
        ]
        + [jax.ShapeDtypeStruct((piece, chans), k) for k in kinds],
        (where, *stats, params, lat, other, near, far_sums, cots),
        scratch=[pltpu.VMEM((half, chans), F32)],
        flops=2 * half * 3 * height * width * chans,
        nbytes=20 * size,
        trans=2 * size,
        name="grad",
    )
    def convolve(far, near_late, far_late, first):
        return call(
            conv_kernel,
            jax.ShapeDtypeStruct((frames, height, width, chans), BF16),
            (where, norm, act, lat, far, near_late, far_late, weight, params, first),
            scratch=[
                pltpu.VMEM((4, height + 2, width, chans), BF16),
                pltpu.VMEM((frames, 3, height, width, chans), F32),
                pltpu.VMEM((7,) + weight.shape[2:], weight.dtype),
                pltpu.SemaphoreType.DMA((7,)),
            ],
            flops=2 * 27 * size * chans,
            nbytes=4 * size + 2 * weight.size,
            trans=2 * size,
            name="conv",
            outside=(7,),
            limit=50 * 1024 * 1024,
        )

    if small:
        got = [
            lax.ppermute(
                p,
                ("dp", "rows"),
                [(z * 4 + r, (z ^ dz) * 4 + (r ^ dr)) for z in range(4) for r in range(4)],
            )
            for p, (dz, dr) in zip(parts[1:], order[1:])
        ]
        near, near_late, total = lax.optimization_barrier((near, near_late, parts[0]))
        far = lax.ppermute(near, "tm", swap)
        far_late = lax.ppermute(near_late, "tm", swap)
        for g in got:
            total = total + g.astype(F32)
        total = total.astype(BF16)
        later, far, far_late, first = lax.optimization_barrier((total, far, far_late, weight[:1, :2]))
        by = [total] + [
            lax.ppermute(t, "dp", [(z, z ^ k) for z in range(4)]) for k, t in ((1, later), (2, total), (3, total))
        ]
        output = convolve(far, near_late, far_late, first)
        *by, output = lax.optimization_barrier((*by, output))
        by = [b.astype(F32) for b in by]
        mine = by[0] + by[2]
        theirs = by[1] + by[3]
        even = clip % 2 == 0
        grad = jnp.concatenate([jnp.where(even, mine, theirs), jnp.where(even, theirs, mine)], axis=0)
    else:
        far = lax.ppermute(near, "tm", swap)
        output = convolve(far, near_late, lax.ppermute(near_late, "tm", swap), weight[:1, :2])
        grad = lax.psum(lax.psum_scatter(parts[0], "rows", scatter_dimension=0, tiled=True), "dp")
    return output[None], grad


def solution(mesh):
    placed = (
        P("dp", "tm", "rows", None, None),
        P(),
        P(),
        P(),
        P(),
        P("dp", "tm", "rows", None, None),
    )
    return jax.shard_map(
        functools.partial(body, mesh.shape["dp"], mesh.shape["rows"]),
        mesh=mesh,
        in_specs=placed,
        out_specs=(P("dp", "tm", "rows", None, None), P(("tm", "rows"), None)),
        check_vma=False,
    )
```

```python
import functools

import jax
import jax.numpy as jnp
from jax import lax
from jax.experimental import pallas as pl
from jax.experimental.pallas import tpu as pltpu
from jax.sharding import PartitionSpec as P

GROUPS = 32
BF16 = jnp.bfloat16
F32 = jnp.float32
VMEM_LIMIT = 24 * 1024 * 1024


def call(kernel, outs, ins, scratch=(), flops=0, nbytes=0, trans=0, name=None, outside=(), limit=VMEM_LIMIT):
    specs = [
        pl.BlockSpec(memory_space=pltpu.HBM if k in outside else pltpu.SMEM if a.dtype == jnp.int32 else pltpu.VMEM)
        for k, a in enumerate(ins)
    ]
    return pl.pallas_call(
        kernel,
        out_shape=outs,
        in_specs=specs,
        out_specs=jax.tree.map(lambda _: pl.BlockSpec(memory_space=pltpu.VMEM), outs),
        scratch_shapes=list(scratch),
        compiler_params=pltpu.CompilerParams(vmem_limit_bytes=limit),
        cost_estimate=pl.CostEstimate(flops=flops, bytes_accessed=nbytes, transcendentals=trans),
        name=name,
    )(*ins)


def channel_sums(ref):
    frames, height, width, chans = ref.shape
    total = jnp.zeros((8, chans), F32)
    squares = jnp.zeros((8, chans), F32)
    for f in range(frames):
        for h in range(height):
            x = ref[f, h].astype(F32).reshape(width // 8, 8, chans)
            total = total + jnp.sum(x, axis=0)
            squares = squares + jnp.sum(x * x, axis=0)
    return jnp.concatenate([total, squares], axis=0)


def own_kernel(own_ref, copy_ref, sums_ref):
    copy_ref[...] = own_ref[...]
    sums_ref[...] = channel_sums(own_ref)


def prep_kernel(where_ref, own_sums_ref, own_ref, other_ref, sums_ref, early_ref, late_ref):
    frames, height, width, chans = own_ref.shape
    is_late = where_ref[0] == 1
    row = where_ref[3]
    sums = own_sums_ref[...] + channel_sums(other_ref)
    sums_ref[...] = sums
    for f in range(frames):
        mine = own_ref[f, row]
        other = other_ref[f, row]
        early_ref[f * width : (f + 1) * width, :] = jnp.where(is_late, other, mine)
        late_ref[f * width : (f + 1) * width, :] = jnp.where(is_late, mine, other)
    for k in range(3):
        term = sums.astype(BF16)
        early_ref[frames * width + 16 * k : frames * width + 16 * (k + 1), :] = term
        sums = sums - term.astype(F32)


def shift_rows(x, by):
    zero = jnp.zeros((1, x.shape[1]), x.dtype)
    if by == 1:
        return jnp.concatenate([x[1:], zero], axis=0)
    if by == -1:
        return jnp.concatenate([zero, x[:-1]], axis=0)
    return x


def cot_kernel(where_ref, own_ref, other_ref, out_ref):
    _, height, width, chans = own_ref.shape
    is_late = where_ref[0] == 1
    for h in range(height):
        a0 = own_ref[0, h].astype(F32)
        a1 = own_ref[1, h].astype(F32)
        b0 = other_ref[0, h].astype(F32)
        b1 = other_ref[1, h].astype(F32)
        first = a0 + b0 + jnp.where(is_late, b1, a1)
        last = jnp.where(is_late, a1, b1)
        high = first.astype(BF16).astype(F32)
        low = first - high
        for term, value in enumerate((high, low, last)):
            for kw in range(3):
                out_ref[kw, term, h] = shift_rows(value, 1 - kw).astype(BF16)


def group_sum(x, per_group):
    chans = x.shape[1]
    lane = lax.broadcasted_iota(jnp.int32, x.shape, 1)
    step = 1
    while step < per_group:
        up = pltpu.roll(x, step, 1)
        down = pltpu.roll(x, chans - step, 1)
        x = x + jnp.where((lane & step) != 0, up, down)
        step *= 2
    return x


def activate(x, scale, shift):
    half = x.astype(F32) * scale + shift
    return half + half * jnp.tanh(half)


def grad_kernel(count, decode, n_stats, n_pieces, rows_out, *refs):
    where_ref = refs[0]
    stats = refs[1 : 1 + n_stats]
    params_ref, own_ref, other_ref, near_ref, far_sums_ref, cots_ref = refs[1 + n_stats : 7 + n_stats]
    act_ref, norm_ref = refs[7 + n_stats : 9 + n_stats]
    pieces = refs[9 + n_stats : 9 + n_stats + n_pieces]
    wg_ref = refs[9 + n_stats + n_pieces]
    late = where_ref[0]
    is_late = late == 1
    frames, height, width, chans = own_ref.shape
    sums = stats[0][...]
    for ref in stats[1:]:
        sums = sums + ref[...]
    if decode:
        for ref, base in ((near_ref, frames * width), (far_sums_ref, 0)):
            terms = [ref[base + 16 * k : base + 16 * (k + 1), :].astype(F32) for k in range(3)]
            sums = sums + (terms[0] + (terms[1] + terms[2]))
    total = jnp.sum(sums[0:8], axis=0, keepdims=True)
    squares = jnp.sum(sums[8:16], axis=0, keepdims=True)
    both = group_sum(jnp.concatenate([total, squares] + [total] * 6, axis=0), chans // GROUPS) / count
    mean = both[0:1]
    var = both[1:2] - mean * mean
    scale = lax.rsqrt(var + 1e-06) * params_ref[0:1, :] * 0.5
    shift = params_ref[1:2, :] * 0.5 - mean * scale
    norm_ref[0:1, :] = scale
    norm_ref[1:2, :] = shift
    norm_ref[2:8, :] = jnp.zeros((6, chans), F32)
    keep = (where_ref[1] != 0).astype(F32)
    for f in range(frames):
        near = near_ref[f * width : (f + 1) * width, :]
        act_ref[f, late * (height + 1)] = (activate(near, scale, shift) * keep).astype(BF16)
        act_ref[f, (1 - late) * (height + 1)] = jnp.zeros((width, chans), BF16)
        for h in range(height):
            x = jnp.where(is_late, other_ref[f, h], own_ref[f, h])
            act_ref[f, h + 1] = activate(x, scale, shift).astype(BF16)

    contract = (((0,), (0,)), ((), ()))
    terms = 3 * height * width

    def stack(kh):
        a0 = act_ref[0, pl.ds(kh, height)].reshape(height * width, chans)
        a1 = act_ref[1, pl.ds(kh, height)].reshape(height * width, chans)
        return jnp.concatenate([a0, a0, a1], axis=0)

    def cots(kw):
        return cots_ref[kw].reshape(terms, chans)

    half = chans // 2
    outer = stack(2 * late)
    base = pl.multiple_of(late * (chans + half), half)
    for kw in range(3):
        wg_ref[pl.ds(base + kw * chans, chans), :] = lax.dot_general(
            outer, cots(kw), contract, preferred_element_type=F32
        )
    middle = stack(1)
    base = pl.multiple_of(3 * chans - late * (5 * half), half)
    wg_ref[pl.ds(base, chans), :] = lax.dot_general(middle, cots(2 * late), contract, preferred_element_type=F32)
    lanes = jnp.where(is_late, middle[:, half:], middle[:, :half])
    base = pl.multiple_of((1 - late) * (4 * chans), half)
    wg_ref[pl.ds(base, half), :] = lax.dot_general(lanes, cots(1), contract, preferred_element_type=F32)
    for k, ref in enumerate(pieces):
        start = pl.multiple_of(where_ref[4 + k], 16)
        ref[...] = wg_ref[pl.ds(start, rows_out), :].astype(ref.dtype)


def conv_kernel(
    where_ref, norm_ref, act_ref, own_ref, far_ref, near_late, far_late, weight_hbm, params_ref, first_ref, out_ref, planes, acc, weight_ref, sems
):
    taps = [(0, 2)] + [(kt, kh) for kt in (1, 2) for kh in range(3)]
    copies = [
        pltpu.make_async_copy(weight_hbm.at[kt, kh], weight_ref.at[k], sems.at[k]) for k, (kt, kh) in enumerate(taps)
    ]
    for c in copies:
        c.start()
    late = where_ref[0]
    frames, height, width, chans = own_ref.shape
    scale = norm_ref[0:1, :]
    shift = norm_ref[1:2, :]
    keep_near = (where_ref[1] != 0).astype(F32)
    keep_far = (where_ref[2] != 0).astype(F32)

    def rim(ref, f, keep):
        return (activate(ref[f * width : (f + 1) * width, :], scale, shift) * keep).astype(BF16)

    @pl.when(late == 0)
    def _():
        for f in range(frames):
            planes[2 + f] = act_ref[f]
            planes[2 + f, height + 1] = rim(far_ref, f, keep_far)
        for k in range(2):
            planes[k] = planes[2]

    @pl.when(late == 1)
    def _():
        for f in range(frames):
            planes[f] = act_ref[f]
            planes[f, 0] = rim(far_ref, f, keep_far)
            planes[2 + f, 0] = rim(far_late, f, keep_far)
            for h in range(height):
                planes[2 + f, h + 1] = activate(own_ref[f, h], scale, shift).astype(BF16)
            planes[2 + f, height + 1] = rim(near_late, f, keep_near)

    early = first_ref.shape[1]
    for kt, offsets in ((0, range(early)), (0, range(early, 3)), (1, range(3)), (2, range(3))):
        first = kt == 0 and offsets[0] == 0
        if not first:
            for kh in offsets:
                copies[3 * kt + kh - early].wait()
        for f in range(frames):
            for kw in range(3):
                total = None
                for kh in offsets:
                    lhs = planes[f + kt, kh : kh + height].reshape(height * width, chans)
                    taps_ref = first_ref.at[0, kh] if first else weight_ref.at[3 * kt + kh - early]
                    part = jnp.dot(lhs, taps_ref[kw], preferred_element_type=F32)
                    total = part if total is None else total + part
                total = total.reshape(height, width, chans)
                acc[f, kw] = total if first else acc[f, kw] + total
    for f in range(frames):
        for h in range(height):
            value = own_ref[f, h].astype(F32) + params_ref[2:3, :]
            value = value + acc[f, 1, h] + shift_rows(acc[f, 0, h], -1) + shift_rows(acc[f, 2, h], 1)
            out_ref[f, h] = value.astype(BF16)


def body(dp, rows, latent, gamma, beta, weight, bias, cotangent):
    nclip, frames, height, width, chans = latent.shape
    lat = latent[0]
    cot = cotangent[0]
    swap = [(0, 1), (1, 0)]
    clip = lax.axis_index("dp")
    late = lax.axis_index("tm")
    band = lax.axis_index("rows")
    count = frames * height * width * (chans // GROUPS) * 2 * rows
    size = frames * height * width * chans
    small = rows == 4 and dp == 4

    joint = [(r, (r + 1) % rows) for r in range(rows)] + [(rows + r, rows + (r - 1) % rows) for r in range(rows)]
    keep_low, keep_high = (band != 0), (band != rows - 1)
    head = [
        late,
        jnp.where(late == 0, keep_low, keep_high),
        jnp.where(late == 0, keep_high, keep_low),
        jnp.where(late == 0, height - 1, 0),
    ]

    other = lax.ppermute(lat, "tm", swap)
    other_cot = lax.ppermute(cot, "tm", swap)
    lat, own_sums = call(
        own_kernel,
        [jax.ShapeDtypeStruct(lat.shape, lat.dtype), jax.ShapeDtypeStruct((16, chans), F32)],
        (lat,),
        flops=3 * size,
        nbytes=4 * size,
        name="own",
    )
    half = 9 * chans // 2
    if small:
        piece = half // 8
        order = [(0, 0), (1, 3), (1, 0), (0, 1), (0, 2), (1, 2), (1, 1), (0, 3)]
        starts = [(band ^ dr) * (2 * piece) + ((clip ^ dz) & 1) * piece for dz, dr in order]
        kinds = [F32] + [BF16] * 7
    else:
        piece = half
        starts = [jnp.int32(0)]
        kinds = [F32]
    where = jnp.stack([jnp.asarray(v).astype(jnp.int32) for v in head + starts])
    sums, early_rims, late_rims = call(
        prep_kernel,
        [
            jax.ShapeDtypeStruct((16, chans), F32),
            jax.ShapeDtypeStruct((frames * width + 48, chans), BF16),
            jax.ShapeDtypeStruct((frames * width, chans), BF16),
        ],
        (where, own_sums, lat, other),
        flops=3 * size,
        nbytes=6 * size,
        name="prep",
    )
    near = lax.ppermute(early_rims, ("tm", "rows"), joint)
    if small:
        stats = [
            sums,
            lax.ppermute(sums, "rows", [(r, (r + 2) % rows) for r in range(rows)]),
        ]
    else:
        stats = [lax.psum(sums, "rows")]
    params = jnp.stack([gamma, beta, bias] + [jnp.zeros_like(bias)] * 5)
    cots = call(
        cot_kernel,
        jax.ShapeDtypeStruct((3, 3, height, width, chans), BF16),
        (where, cot, other_cot),
        flops=10 * size,
        nbytes=14 * size,
        name="cots",
    )
    cots, params, late_rims, stats[-1] = lax.optimization_barrier((cots, params, late_rims, stats[-1]))
    near_late = lax.ppermute(late_rims, ("tm", "rows"), joint)
    near, stats[-1], cots = lax.optimization_barrier((near, stats[-1], cots))
    far_sums = lax.ppermute(near[frames * width :], "tm", swap)
    act, norm, *parts = call(
        functools.partial(grad_kernel, count, small, len(stats), len(kinds), piece),
        [
            jax.ShapeDtypeStruct((frames, height + 2, width, chans), BF16),
            jax.ShapeDtypeStruct((8, chans), F32),
        ]
        + [jax.ShapeDtypeStruct((piece, chans), k) for k in kinds],
        (where, *stats, params, lat, other, near, far_sums, cots),
        scratch=[pltpu.VMEM((half, chans), F32)],
        flops=2 * half * 3 * height * width * chans,
        nbytes=20 * size,
        trans=2 * size,
        name="grad",
    )
    def convolve(far, near_late, far_late, first):
        return call(
            conv_kernel,
            jax.ShapeDtypeStruct((frames, height, width, chans), BF16),
            (where, norm, act, lat, far, near_late, far_late, weight, params, first),
            scratch=[
                pltpu.VMEM((4, height + 2, width, chans), BF16),
                pltpu.VMEM((frames, 3, height, width, chans), F32),
                pltpu.VMEM((7,) + weight.shape[2:], weight.dtype),
                pltpu.SemaphoreType.DMA((7,)),
            ],
            flops=2 * 27 * size * chans,
            nbytes=4 * size + 2 * weight.size,
            trans=2 * size,
            name="conv",
            outside=(7,),
            limit=50 * 1024 * 1024,
        )

    if small:
        got = [
            lax.ppermute(
                p,
                ("dp", "rows"),
                [(z * 4 + r, (z ^ dz) * 4 + (r ^ dr)) for z in range(4) for r in range(4)],
            )
            for p, (dz, dr) in zip(parts[1:], order[1:])
        ]
        near, near_late, total = lax.optimization_barrier((near, near_late, parts[0]))
        far = lax.ppermute(near, "tm", swap)
        far_late = lax.ppermute(near_late, "tm", swap)
        for g in got:
            total = total + g.astype(F32)
        total = total.astype(BF16)
        later, far, far_late, first = lax.optimization_barrier((total, far, far_late, weight[:1, :2]))
        by = [total] + [
            lax.ppermute(t, "dp", [(z, z ^ k) for z in range(4)]) for k, t in ((1, later), (2, total), (3, total))
        ]
        output = convolve(far, near_late, far_late, first)
        *by, output = lax.optimization_barrier((*by, output))
        by = [b.astype(F32) for b in by]
        mine = by[0] + by[2]
        theirs = by[1] + by[3]
        even = clip % 2 == 0
        grad = jnp.concatenate([jnp.where(even, mine, theirs), jnp.where(even, theirs, mine)], axis=0)
    else:
        far = lax.ppermute(near, "tm", swap)
        output = convolve(far, near_late, lax.ppermute(near_late, "tm", swap), weight[:1, :2])
        grad = lax.psum(lax.psum_scatter(parts[0], "rows", scatter_dimension=0, tiled=True), "dp")
    return output[None], grad


def solution(mesh):
    placed = (
        P("dp", "tm", "rows", None, None),
        P(),
        P(),
        P(),
        P(),
        P("dp", "tm", "rows", None, None),
    )
    return jax.shard_map(
        functools.partial(body, mesh.shape["dp"], mesh.shape["rows"]),
        mesh=mesh,
        in_specs=placed,
        out_specs=(P("dp", "tm", "rows", None, None), P(("tm", "rows"), None)),
        check_vma=False,
    )
```
